32 devices in a mesh: row: 16 (over z, y, core), col: 2 (over x).
Axes of the slice: x: 2, y: 2, z: 4, core: 2. Of those that a mesh axis runs over, the one named last changes fastest.
Arguments:
- pair: bfloat16 [64, 128, 128], P(None, 'row', 'col'), may hold values from -18 to 18
- dilations: int32 [2], replicated, may hold values from 1 to 4, as said below
- mask: int32 [128], replicated, may hold values from 0 to 1, as said below
- labels: int32 [128, 128], P('row', 'col'), may hold values from 0 to 36, as said below
- conv_first: bfloat16 [9, 64, 64], replicated, may hold values from -0.25 to 0.25
- conv_second: bfloat16 [9, 64, 64], replicated, may hold values from -0.25 to 0.25
- norm_gain: float32 [2, 64], replicated, may hold values from 0.1 to 1.9
- norm_shift: float32 [2, 64], replicated, may hold values from -3 to 3
- head_weight: bfloat16 [64, 37], replicated, may hold values from -25 to 25
- head_bias: float32 [37], replicated, may hold values from -4 to 4
Outputs:
- loss: float32 [], replicated
- grad_head: float32 [64, 37], replicated
- grad_bias: float32 [37], replicated
- grad_norm: float32 [2, 64], replicated
- grad_conv: float32 [9, 64, 64], replicated
- act_grad: bfloat16 [64, 128, 128], P(None, 'row', 'col')
The draws below stay inside these ranges and needn't reach their ends.
Inputs may be any that keep to these rules, and one draw needn't show every extreme that they name: `dilations`: one of the two entries is 4. `mask`: residue 0 is valid. labels[i, j] == labels[j, i].
All inputs are finite; a program needn't handle non-finite values.
Results may differ from the reference program's by a relative error of at most 0.0094.
Values may be sent and summed in bfloat16 or wider, within the bound.
A program may use at most 64 MiB of HBM per device.

```python
import jax
import jax.numpy as jnp
from jax import lax

C = 64
BINS = 37
DMAX = 4
L = 128


def draw_pair(key, part):
    key = jax.random.fold_in(key, 11)
    noise_key, offset_key = jax.random.split(key)
    position = jnp.arange(L, dtype=jnp.float32) / L
    noise_field = jnp.clip(jax.random.normal(noise_key, (C, L, L), jnp.float32), -4.0, 4.0)
    offset = 0.8 * jnp.clip(jax.random.normal(offset_key, (C, 1, 1), jnp.float32), -2.0, 2.0)
    rising = 1.0 + position[:, None] + position[None, :]
    return ((noise_field + offset) * rising).astype(jnp.bfloat16)


def draw_head_weight(key, part):
    key = jax.random.fold_in(key, 12)
    base_weight = jnp.clip(jax.random.normal(key, (C, BINS), jnp.float32), -4.0, 4.0) * (3.0 * C ** (-0.5))
    return base_weight.astype(jnp.bfloat16)


def draw_dilations(key, part):
    key = jax.random.fold_in(key, 13)
    rate_key, place_key = jax.random.split(key)
    other_rate = jax.random.randint(rate_key, (), 1, DMAX + 1, dtype=jnp.int32)
    chosen = jax.random.randint(place_key, (), 0, 2, dtype=jnp.int32)
    return jnp.where(jnp.arange(2, dtype=jnp.int32) == chosen, jnp.int32(DMAX), other_rate).astype(jnp.int32)


def draw_mask(key, part):
    key = jax.random.fold_in(key, 14)
    length_key, gap_key = jax.random.split(key)
    valid_length = jax.random.randint(length_key, (), 3 * L // 4, L + 1, dtype=jnp.int32)
    gap_draw = jax.random.randint(gap_key, (L,), 0, 20, dtype=jnp.int32)
    position = jnp.arange(L, dtype=jnp.int32)
    keep = (position < valid_length) & ((gap_draw != 0) | (position == 0))
    return keep.astype(jnp.int32)


def draw_labels(key, part):
    key = jax.random.fold_in(key, 15)
    upper_draw = jax.random.randint(key, (L, L), 0, BINS, dtype=jnp.int32)
    position = jnp.arange(L, dtype=jnp.int32)
    return jnp.where(position[:, None] <= position[None, :], upper_draw, upper_draw.T).astype(jnp.int32)


def noise(key, shape, width, most, kind=jnp.bfloat16):
    array = width * jax.random.normal(key, shape, jnp.float32)
    return jnp.clip(array, min=-most, max=most).astype(kind)


def setup_inputs(seed: int = 0) -> dict:
    arg_keys = jax.random.split(jax.random.key(seed), 11)
    return {
        "pair": draw_pair(jax.random.fold_in(arg_keys[10], 71), 0),
        "dilations": draw_dilations(jax.random.fold_in(arg_keys[10], 71), 0),
        "mask": draw_mask(jax.random.fold_in(arg_keys[10], 71), 0),
        "labels": draw_labels(jax.random.fold_in(arg_keys[10], 71), 0),
        "conv_first": noise(arg_keys[4], (9, C, C), (9 * C) ** -0.5, 0.25),
        "conv_second": noise(arg_keys[5], (9, C, C), (9 * C) ** -0.5, 0.25),
        "norm_gain": jnp.clip(1.0 + 0.18 * jax.random.normal(arg_keys[6], (2, C), jnp.float32), 0.1, 1.9),
        "norm_shift": noise(arg_keys[7], (2, C), 0.5, 3.0, jnp.float32),
        "head_weight": draw_head_weight(jax.random.fold_in(arg_keys[10], 71), 0),
        "head_bias": noise(arg_keys[9], (BINS,), 1.0, 4.0, jnp.float32),
    }


EPSILON = 1e-05

def padded_map(field_tile):
    return jnp.pad(field_tile, ((0, 0), (DMAX, DMAX), (DMAX, DMAX)))

def dilated(padded, weight, dilation, direction):
    in_chans = padded.shape[0]
    out_chans = weight.shape[1]
    map_side = padded.shape[1] - 2 * DMAX
    block_rows = min(map_side, 256)

    def one_block(block_index):
        first_row = block_index * block_rows
        accumulated = jnp.zeros((out_chans, block_rows * map_side), jnp.float32)
        for tap_index in range(9):
            offset_down = tap_index // 3 - 1
            offset_right = tap_index % 3 - 1
            start_at = (jnp.int32(0), first_row + DMAX + direction * offset_down * dilation, jnp.int32(DMAX) + direction * offset_right * dilation)
            window_piece = lax.dynamic_slice(padded, start_at, (in_chans, block_rows, map_side))
            kernel = weight[tap_index] if direction > 0 else weight[tap_index].T
            accumulated = accumulated + jnp.dot(kernel, window_piece.reshape(in_chans, block_rows * map_side), preferred_element_type=jnp.float32)
        return accumulated.reshape(out_chans, block_rows, map_side)
    blocks = lax.map(one_block, jnp.arange(map_side // block_rows, dtype=jnp.int32))
    return blocks.transpose(1, 0, 2, 3).reshape(out_chans, map_side, map_side)

def kernel_grad(padded, upstream, dilation):
    in_chans = padded.shape[0]
    out_chans = upstream.shape[0]
    map_side = upstream.shape[1]
    block_rows = min(map_side, 256)

    def one_block(block_index):
        first_row = block_index * block_rows
        upper = lax.dynamic_slice(upstream, (jnp.int32(0), first_row, jnp.int32(0)), (out_chans, block_rows, map_side))
        flat_up = upper.reshape(out_chans, block_rows * map_side)
        tap_terms = []
        for tap_index in range(9):
            offset_down = tap_index // 3 - 1
            offset_right = tap_index % 3 - 1
            start_at = (jnp.int32(0), first_row + DMAX + offset_down * dilation, jnp.int32(DMAX) + offset_right * dilation)
            window_piece = lax.dynamic_slice(padded, start_at, (in_chans, block_rows, map_side))
            tap_terms.append(lax.dot_general(flat_up, window_piece.reshape(in_chans, block_rows * map_side), (((1,), (1,)), ((), ())), preferred_element_type=jnp.float32))
        return jnp.stack(tap_terms)
    blocks = lax.map(one_block, jnp.arange(map_side // block_rows, dtype=jnp.int32))
    return lax.optimization_barrier(jnp.sum(blocks, axis=0))

def channel_moments(hidden, pair_mask, count):
    mean_value = lax.optimization_barrier(jnp.sum(pair_mask[None] * hidden, axis=(1, 2))) / count
    centered = hidden - mean_value[:, None, None]
    variance = lax.optimization_barrier(jnp.sum(pair_mask[None] * centered * centered, axis=(1, 2))) / count
    return (mean_value, variance)

def reference(pair, dilations, mask, labels, conv_first, conv_second, norm_gain, norm_shift, head_weight, head_bias):
    mask_float = mask.astype(jnp.float32)
    valid_total = jnp.sum(mask_float)
    count = valid_total * valid_total
    pair_mask = mask_float[:, None] * mask_float[None, :]
    hidden_one = dilated(padded_map(pair), conv_first, dilations[0], 1)
    mean_one, var_one = channel_moments(hidden_one, pair_mask, count)
    normed_one = norm_gain[0][:, None, None] * (hidden_one - mean_one[:, None, None]) / jnp.sqrt(var_one + EPSILON)[:, None, None] + norm_shift[0][:, None, None]
    activation = (pair_mask[None] * jax.nn.elu(normed_one)).astype(jnp.bfloat16)
    padded_act = padded_map(activation)
    hidden_two = dilated(padded_act, conv_second, dilations[1], 1)
    mean_two, var_two = channel_moments(hidden_two, pair_mask, count)
    inverse_two = 1.0 / jnp.sqrt(var_two + EPSILON)
    normal_two = (hidden_two - mean_two[:, None, None]) * inverse_two[:, None, None]
    summed = norm_gain[1][:, None, None] * normal_two + norm_shift[1][:, None, None] + pair.astype(jnp.float32)
    output = (pair_mask[None] * jax.nn.elu(summed)).astype(jnp.bfloat16)
    flat_out = output.reshape(C, L * L)
    logits = (lax.dot_general(head_weight, flat_out, (((0,), (0,)), ((), ())), preferred_element_type=jnp.float32) + head_bias[:, None]).reshape(BINS, L, L)
    scores = 0.5 * (logits + logits.transpose(0, 2, 1))
    top_score = lax.optimization_barrier(jnp.max(scores, axis=0))
    log_total = top_score + jnp.log(lax.optimization_barrier(jnp.sum(jnp.exp(scores - top_score[None]), axis=0)))
    one_hot = (labels[None, :, :] == jnp.arange(BINS, dtype=jnp.int32)[:, None, None]).astype(jnp.float32)
    picked = lax.optimization_barrier(jnp.sum(one_hot * scores, axis=0))
    loss = jnp.sum(pair_mask * (log_total - picked)) / count
    logit_grad = pair_mask[None] * (jnp.exp(scores - log_total[None]) - one_hot)
    symmetric_grad = 0.5 * (logit_grad + logit_grad.transpose(0, 2, 1))
    logit_half = symmetric_grad.astype(jnp.bfloat16).reshape(BINS, L * L)
    grad_head = lax.dot_general(flat_out, logit_half, (((1,), (1,)), ((), ())), preferred_element_type=jnp.float32) / L
    grad_bias = lax.optimization_barrier(jnp.sum(symmetric_grad, axis=(1, 2))) / L
    output_grad = jnp.dot(head_weight, logit_half, preferred_element_type=jnp.float32).reshape(C, L, L)
    summed_grad = output_grad * pair_mask[None] * jnp.where(summed > 0, 1.0, jnp.exp(jnp.minimum(summed, 0.0)))
    scale_sum = lax.optimization_barrier(jnp.sum(summed_grad * normal_two, axis=(1, 2)))
    shift_sum = lax.optimization_barrier(jnp.sum(summed_grad, axis=(1, 2)))
    grad_norm = jnp.stack([scale_sum, shift_sum]) / L
    pre_grad = pair_mask[None] * (norm_gain[1] * inverse_two)[:, None, None] * (summed_grad - (shift_sum / count)[:, None, None] - normal_two * (scale_sum / count)[:, None, None])
    pre_half = pre_grad.astype(jnp.bfloat16)
    grad_conv = kernel_grad(padded_act, pre_half, dilations[1]) / L
    act_grad = dilated(padded_map(pre_half), conv_second, dilations[1], -1).astype(jnp.bfloat16)
    return (loss, grad_head, grad_bias, grad_norm, grad_conv, act_grad)
```

```python
import functools

import jax
import jax.numpy as jnp
from jax import lax
from jax.experimental import pallas as pl
from jax.experimental.pallas import tpu as pltpu
from jax.sharding import PartitionSpec as P

EPSILON = 1e-05
LANES = 128
MESH = pl.DeviceIdType.MESH
F32 = jnp.float32
BF16 = jnp.bfloat16
NT = (((1,), (1,)), ((), ()))
DIRECTIONS = tuple((a, b) for a in (-1, 0, 1) for b in (-1, 0, 1) if (a, b) != (0, 0))


def elu(v):
    return jnp.where(v > 0, v, jnp.exp(jnp.minimum(v, 0.0)) - 1.0)


def split_of(n):
    group = 2 if n < 40 else 1
    return group, 40 // group


def kernel(
    sizes, dil, pair, rowm, colm, lab, w1, w2, par, hw, hb,
    act_out, gsum_out, tail_out,
    pb, pf, h1, a1, h2, du, dh, yb, zb, zr, zt, st1, st2, st3, part, gath, red,
    halo_s, halo_r, send_s, recv_s,
):
    R, W, C, nr, nc = sizes
    n = nr * nc
    q = W // R
    group, owners = split_of(n)
    row = lax.axis_index("row")
    col = lax.axis_index("col")
    me = row * nc + col
    my_owner = (me * owners + n - 1) // n
    is_owner = jnp.logical_and(my_owner < owners, (my_owner * n) // owners == me)

    def device(p):
        return (p // nc, p % nc)

    def to_all(slots):
        def step(k, carry):
            pltpu.make_async_remote_copy(
                src_ref=slots[0], dst_ref=slots[0], send_sem=slots[1], recv_sem=slots[2],
                device_id=device((me + k) % n), device_id_type=MESH,
            ).start()
            return carry

        lax.fori_loop(1, n, step, 0)

    def wait_bytes(ref, sem):
        pltpu.make_async_copy(ref, ref, sem).wait()

    def halo_copy(phase, index, src, src_at, dst, dst_at, width):
        dr, dc = DIRECTIONS[index]
        hr, hc = width

        def span(delta, edge, length, src_zero, dst_zero):
            if delta == 0:
                return pl.ds(src_zero, length), pl.ds(dst_zero, length)
            if delta > 0:
                return pl.ds(src_zero + length - edge, edge), pl.ds(dst_zero - edge, edge)
            return pl.ds(src_zero, edge), pl.ds(dst_zero + length, edge)

        sr, tr = span(dr, hr, R, src_at[0], dst_at[0])
        sc, tc = span(dc, hc, W, src_at[1], dst_at[1])
        return pltpu.make_async_remote_copy(
            src_ref=src.at[sr, sc, :], dst_ref=dst.at[tr, tc, :],
            send_sem=halo_s.at[phase, index], recv_sem=halo_r.at[phase, index],
            device_id=(row + dr, col + dc), device_id_type=MESH,
        )

    def inside(r, c):
        return (r >= 0) & (r < nr) & (c >= 0) & (c < nc)

    def halo_start(*spec):
        for index, (dr, dc) in enumerate(DIRECTIONS):
            @pl.when(inside(row + dr, col + dc))
            def _():
                halo_copy(spec[0], index, *spec[1:]).start()

    def halo_recv(*spec):
        for index, (dr, dc) in enumerate(DIRECTIONS):
            @pl.when(inside(row - dr, col - dc))
            def _():
                halo_copy(spec[0], index, *spec[1:]).wait_recv()

    def halo_sent(*spec):
        for index, (dr, dc) in enumerate(DIRECTIONS):
            @pl.when(inside(row + dr, col + dc))
            def _():
                halo_copy(spec[0], index, *spec[1:]).wait_send()

    def blocks(count, body):
        if count == 1:
            body(0)
        else:
            def step(k, carry):
                body(pl.multiple_of(k * 8, 8))
                return carry

            lax.fori_loop(0, count, step, 0)

    def pmask(first, lanes):
        return rowm[pl.ds(first + 4, 8), :, :lanes] * colm[8 : 8 + W, :lanes][None]

    def window(ref, r, c, cols):
        return ref[pl.ds(r, 8), pl.ds(c, cols), :].astype(BF16).reshape(8 * cols, C)

    taps = [(a, b) for a in (-1, 0, 1) for b in (-1, 0, 1)]
    inv_count = par[4:5, :]

    barrier = pltpu.get_barrier_semaphore()

    def greet(k, carry):
        pl.semaphore_signal(barrier, inc=1, device_id=device((me + k) % n), device_id_type=MESH)
        return carry

    pb[...] = jnp.zeros_like(pb)
    h2[...] = jnp.zeros_like(h2)
    du[...] = jnp.zeros_like(du)
    lax.fori_loop(1, n, greet, 0)
    pl.semaphore_wait(barrier, n - 1)

    pair_spec = (0, pair, (0, 0), pb, (8, 16), (8, 16))
    halo_start(*pair_spec)
    pb[8 : 8 + R, 16 : 16 + W, :] = pair[...]
    halo_recv(*pair_spec)
    pf[...] = pb[...].astype(F32)

    d0 = dil[0]
    d1 = dil[1]

    def first_conv(r):
        total = None
        for t, (a, b) in enumerate(taps):
            x = window(pf, r + 4 + a * d0, 8 + b * d0, W + 16)
            term = lax.dot_general(x, w1[t], NT, preferred_element_type=F32)
            total = term if total is None else total + term
        h1[pl.ds(r, 8)] = total.reshape(8, W + 16, C)

    blocks((R + 8) // 8, first_conv)

    def moments(ref, slots, phase):
        def body(first, r):
            h = ref[pl.ds(4 + r, 8), 8 : 8 + W, :]
            mh = pmask(r, C) * h
            s1 = jnp.sum(mh.reshape(8 * W, C), axis=0, keepdims=True)
            s2 = jnp.sum((mh * h).reshape(8 * W, C), axis=0, keepdims=True)
            value = jnp.concatenate([s1, s2], axis=1)
            slots[me] = value if first else slots[me] + value

        body(True, 0)
        if R > 8:
            lax.fori_loop(1, R // 8, lambda k, z: (body(False, pl.multiple_of(k * 8, 8)), z)[1], 0)
        to_all((slots.at[me], send_s.at[phase], recv_s.at[phase]))

    def gathered(slots, phase):
        wait_bytes(slots.at[pl.ds(0, n - 1)], recv_s.at[phase])
        return jnp.sum(slots[...], axis=0)

    def mean_inverse(sums):
        mean = sums[:, :C] * inv_count
        var = sums[:, C:] * inv_count - mean * mean
        return mean, 1.0 / jnp.sqrt(var + EPSILON)

    moments(h1, st1, 0)
    mean1, inv1 = mean_inverse(gathered(st1, 0))
    scale1 = par[0:1, :] * inv1
    shift1 = par[1:2, :] - mean1 * scale1

    def first_act(r):
        v = h1[pl.ds(r, 8)] * scale1[None] + shift1[None]
        m = rowm[pl.ds(r, 8), :, :C] * colm[:, :C][None]
        a1[pl.ds(r, 8)] = (m * elu(v)).astype(BF16).astype(F32)

    blocks((R + 8) // 8, first_act)

    def second_conv(r):
        total = None
        for t, (a, b) in enumerate(taps):
            x = window(a1, r + 4 + a * d1, 8 + b * d1, W)
            term = lax.dot_general(x, w2[t], NT, preferred_element_type=F32)
            total = term if total is None else total + term
        h2[pl.ds(4 + r, 8), 8 : 8 + W, :] = total.reshape(8, W, C)

    blocks(R // 8, second_conv)
    moments(h2, st2, 1)
    h2_spec = (1, h2, (4, 8), h2, (4, 8), (4, 8))
    halo_start(*h2_spec)
    mean2, inv2 = mean_inverse(gathered(st2, 1))
    gain2 = par[2:3, :]

    def features(r):
        xhat = (h2[pl.ds(4 + r, 8), 8 : 8 + W, :] - mean2[None]) * inv2[None]
        u = gain2[None] * xhat + par[3:4, :][None] + pf[pl.ds(8 + r, 8), 16 : 16 + W, :]
        return xhat, u

    def head(r):
        _, u = features(r)
        y = (pmask(r, C) * elu(u)).astype(BF16).reshape(8 * W, C)
        z = jnp.dot(y, hw[...], preferred_element_type=F32) + hb[...]
        yb[pl.ds(r, 8)] = y.reshape(8, W, C)
        zb[pl.ds(r, 8)] = z.reshape(8, W, LANES)

    blocks(R // 8, head)

    has_self = row // q == col
    mine = row % q

    def mirror_copy(b):
        return pltpu.make_async_remote_copy(
            src_ref=zb.at[:, pl.ds(b * R, R), :], dst_ref=zr.at[mine],
            send_sem=send_s.at[2], recv_sem=recv_s.at[2],
            device_id=(col * q + b, row // q), device_id_type=MESH,
        )

    for b in range(q):
        stays = has_self & (mine == b)

        @pl.when(jnp.logical_not(stays))
        def _():
            mirror_copy(b).start()

        @pl.when(stays)
        def _():
            zr[b] = zb[:, b * R : (b + 1) * R, :]

    @pl.when(has_self)
    def _():
        wait_bytes(zr.at[pl.ds(0, q - 1)], recv_s.at[2])

    @pl.when(jnp.logical_not(has_self))
    def _():
        wait_bytes(zr, recv_s.at[2])

    for b in range(q):
        zt[:, b * R : (b + 1) * R, :] = jnp.swapaxes(zr[b], 0, 1)

    def loss_part(first, r):
        s = 0.5 * (zb[pl.ds(r, 8)] + zt[pl.ds(r, 8)])
        top = jnp.max(s, axis=2, keepdims=True)
        log_total = top + jnp.log(jnp.sum(jnp.exp(s - top), axis=2, keepdims=True))
        bins = lax.broadcasted_iota(jnp.int32, (8, W, LANES), 2)
        hot = bins == lab[pl.ds(r, 8)]
        m = pmask(r, LANES)
        lossy = m * jnp.where(hot, log_total - s, 0.0)
        g = m * (jnp.exp(s - log_total) - jnp.where(hot, 1.0, 0.0))
        gh = g.astype(BF16).reshape(8 * W, LANES)
        y = yb[pl.ds(r, 8)].reshape(8 * W, C)
        head_part = jnp.dot(y.astype(F32).T.astype(BF16), gh, preferred_element_type=F32)
        dy = lax.dot_general(gh, hw[...], NT, preferred_element_type=F32).reshape(8, W, C)
        xhat, u = features(r)
        grad = dy * pmask(r, C) * jnp.where(u > 0, 1.0, jnp.exp(jnp.minimum(u, 0.0)))
        du[pl.ds(4 + r, 8), 8 : 8 + W, :] = grad
        s1 = jnp.sum((grad * xhat).reshape(8 * W, C), axis=0, keepdims=True)
        s2 = jnp.sum(grad.reshape(8 * W, C), axis=0, keepdims=True)
        bias = jnp.sum(g.reshape(8 * W, LANES), axis=0, keepdims=True)
        loss = jnp.sum(lossy.reshape(8 * W, LANES), axis=0, keepdims=True)
        value = jnp.concatenate(
            [jnp.concatenate([s1, s2], axis=1), bias, loss, jnp.zeros_like(loss)], axis=0
        )
        last = jnp.concatenate([jnp.zeros((C, C), F32), head_part[:, :C]], axis=1)
        last = last.reshape(8, 8, LANES)
        if first:
            st3[me] = value
            part[32:40] = last
        else:
            st3[me] = st3[me] + value
            part[32:40] = part[32:40] + last

    loss_part(True, 0)
    if R > 8:
        lax.fori_loop(
            1, R // 8, lambda k, z: (loss_part(False, pl.multiple_of(k * 8, 8)), z)[1], 0
        )
    to_all((st3.at[me], send_s.at[3], recv_s.at[3]))
    du_spec = (2, du, (4, 8), du, (4, 8), (4, 8))
    halo_start(*du_spec)
    halo_recv(*h2_spec)
    halo_recv(*du_spec)
    sums3 = gathered(st3, 3)
    tail_out[...] = sums3
    scale_mean = sums3[0:1, :C] * inv_count
    shift_mean = sums3[0:1, C:] * inv_count
    back = gain2 * inv2

    def second_grad(r):
        m = rowm[pl.ds(r, 8), :, :C] * colm[:, :C][None]
        xhat = (h2[pl.ds(r, 8)] - mean2[None]) * inv2[None]
        v = m * back[None] * (du[pl.ds(r, 8)] - shift_mean[None] - xhat * scale_mean[None])
        dh[pl.ds(r, 8)] = v.astype(BF16).astype(F32)

    blocks((R + 8) // 8, second_grad)

    def weight_grad(first, r):
        d = dh[pl.ds(4 + r, 8), 8 : 8 + W, :].reshape(8 * W, C)
        dt = d.T.astype(BF16)
        terms = []
        for a, b in taps:
            x = window(a1, r + 4 + a * d1, 8 + b * d1, W)
            terms.append(jnp.dot(dt, x, preferred_element_type=F32))
        terms.append(jnp.zeros((C, C), F32))
        for k in range(5):
            value = jnp.concatenate(terms[2 * k : 2 * k + 2], axis=1).reshape(8, 8, LANES)
            if first and k < 4:
                part[8 * k : 8 * k + 8] = value
            else:
                part[8 * k : 8 * k + 8] = part[8 * k : 8 * k + 8] + value

    weight_grad(True, 0)
    if R > 8:
        lax.fori_loop(
            1, R // 8, lambda k, z: (weight_grad(False, pl.multiple_of(k * 8, 8)), z)[1], 0
        )

    def scatter(k, carry):
        target = (k * n) // owners

        @pl.when(target != me)
        def _():
            pltpu.make_async_remote_copy(
                src_ref=part.at[pl.ds(k * group, group)], dst_ref=gath.at[me],
                send_sem=send_s.at[4], recv_sem=recv_s.at[4],
                device_id=device(target), device_id_type=MESH,
            ).start()

        @pl.when(target == me)
        def _():
            gath[me] = part[pl.ds(k * group, group)]

        return carry

    lax.fori_loop(0, owners, scatter, 0)

    def input_grad(r):
        total = None
        for t, (a, b) in enumerate(taps):
            x = window(dh, r + 4 - a * d1, 8 - b * d1, W)
            term = jnp.dot(x, w2[t], preferred_element_type=F32)
            total = term if total is None else total + term
        act_out[pl.ds(r, 8)] = total.reshape(8, W, C).astype(BF16)

    blocks(R // 8, input_grad)

    @pl.when(is_owner)
    def _():
        wait_bytes(gath.at[pl.ds(0, n - 1)], recv_s.at[4])
        red[pl.ds(my_owner * group, group)] = jnp.sum(gath[...], axis=0)
        mine_red = red.at[pl.ds(my_owner * group, group)]
        to_all((mine_red, send_s.at[5], recv_s.at[5]))
        wait_bytes(red.at[pl.ds(0, (owners - 1) * group)], recv_s.at[5])

    @pl.when(jnp.logical_not(is_owner))
    def _():
        wait_bytes(red, recv_s.at[5])

    gsum_out[...] = red[...]

    halo_sent(*pair_spec)
    halo_sent(*h2_spec)
    halo_sent(*du_spec)
    wait_bytes(st1.at[pl.ds(0, n - 1)], send_s.at[0])
    wait_bytes(st2.at[pl.ds(0, n - 1)], send_s.at[1])
    wait_bytes(st3.at[pl.ds(0, n - 1)], send_s.at[3])

    @pl.when(has_self)
    def _():
        wait_bytes(zr.at[pl.ds(0, q - 1)], send_s.at[2])

    @pl.when(jnp.logical_not(has_self))
    def _():
        wait_bytes(zr, send_s.at[2])

    @pl.when(is_owner)
    def _():
        wait_bytes(part.at[pl.ds(0, (owners - 1) * group)], send_s.at[4])
        wait_bytes(gath.at[pl.ds(0, n - 1)], send_s.at[5])

    @pl.when(jnp.logical_not(is_owner))
    def _():
        wait_bytes(part, send_s.at[4])


def body(
    pair, dilations, mask, labels, conv_first, conv_second,
    norm_gain, norm_shift, head_weight, head_bias,
):
    C, R, W = pair.shape
    K = head_weight.shape[1]
    nr, nc = lax.axis_size("row"), lax.axis_size("col")
    n = nr * nc
    group, owners = split_of(n)
    extent = R * nr
    mask_float = mask.astype(F32)
    valid = jnp.sum(mask_float)
    count = valid * valid
    padded = jnp.pad(mask_float, (8, 8))
    rows = lax.dynamic_slice_in_dim(padded, lax.axis_index("row") * R + 4, R + 8)
    cols = lax.dynamic_slice_in_dim(padded, lax.axis_index("col") * W, W + 16)
    rowm = jnp.broadcast_to(rows[:, None, None], (R + 8, 1, LANES))
    colm = jnp.broadcast_to(cols[:, None], (W + 16, LANES))
    par = jnp.concatenate(
        [
            jnp.stack([norm_gain[0], norm_shift[0], norm_gain[1], norm_shift[1]]),
            jnp.broadcast_to(1.0 / count, (4, C)),
        ]
    )
    hw = jnp.pad(head_weight, ((0, 0), (0, LANES - K)))
    hb = jnp.pad(head_bias[None], ((0, 0), (0, LANES - K)), constant_values=-1e30)
    vmem = pl.BlockSpec(memory_space=pltpu.VMEM)
    smem = pl.BlockSpec(memory_space=pltpu.SMEM)
    ring = (R + 8, W + 16, C)
    act, gsum, tail = pl.pallas_call(
        functools.partial(kernel, (R, W, C, nr, nc)),
        out_shape=(
            jax.ShapeDtypeStruct((R, W, C), BF16),
            jax.ShapeDtypeStruct((40, 8, LANES), F32),
            jax.ShapeDtypeStruct((4, LANES), F32),
        ),
        in_specs=[smem] + [vmem] * 9,
        out_specs=(vmem, vmem, vmem),
        scratch_shapes=[
            pltpu.VMEM((R + 16, W + 32, C), BF16),
            pltpu.VMEM((R + 16, W + 32, C), F32),
            pltpu.VMEM(ring, F32),
            pltpu.VMEM(ring, F32),
            pltpu.VMEM(ring, F32),
            pltpu.VMEM(ring, F32),
            pltpu.VMEM(ring, F32),
            pltpu.VMEM((R, W, C), BF16),
            pltpu.VMEM((R, W, LANES), F32),
            pltpu.VMEM((W // R, R, R, LANES), F32),
            pltpu.VMEM((R, W, LANES), F32),
            pltpu.VMEM((n, 1, LANES), F32),
            pltpu.VMEM((n, 1, LANES), F32),
            pltpu.VMEM((n, 4, LANES), F32),
            pltpu.VMEM((40, 8, LANES), F32),
            pltpu.VMEM((n, group, 8, LANES), F32),
            pltpu.VMEM((40, 8, LANES), F32),
            pltpu.SemaphoreType.DMA((3, 8)),
            pltpu.SemaphoreType.DMA((3, 8)),
            pltpu.SemaphoreType.DMA((6,)),
            pltpu.SemaphoreType.DMA((6,)),
        ],
        compiler_params=pltpu.CompilerParams(
            collective_id=0, has_side_effects=True, vmem_limit_bytes=56 * 1024 * 1024
        ),
    )(
        dilations, pair.transpose(1, 2, 0), rowm, colm, labels[:, :, None],
        conv_first, conv_second, par, hw, hb,
    )
    grads = gsum.reshape(5, C, 2, C).transpose(0, 2, 1, 3).reshape(10, C, C) / extent
    return (
        jnp.sum(tail[2]) / count,
        grads[9][:, :K],
        tail[1, :K] / extent,
        tail[0].reshape(2, C) / extent,
        grads[:9],
        act.transpose(2, 0, 1),
    )


def solution(mesh):
    placed = (P(None, "row", "col"), P(), P(), P("row", "col"), P(), P(), P(), P(), P(), P())
    return jax.shard_map(
        body,
        mesh=mesh,
        in_specs=placed,
        out_specs=(P(), P(), P(), P(), P(), P(None, "row", "col")),
        check_vma=False,
    )
```

```python
import functools

import jax
import jax.numpy as jnp
from jax import lax
from jax.experimental import pallas as pl
from jax.experimental.pallas import tpu as pltpu
from jax.sharding import PartitionSpec as P

EPSILON = 1e-05
LANES = 128
MESH = pl.DeviceIdType.MESH
F32 = jnp.float32
BF16 = jnp.bfloat16
NT = (((1,), (1,)), ((), ()))
DIRECTIONS = tuple((a, b) for a in (-1, 0, 1) for b in (-1, 0, 1) if (a, b) != (0, 0))


def elu(v):
    return jnp.where(v > 0, v, jnp.exp(jnp.minimum(v, 0.0)) - 1.0)


GROUP, OWNERS = 2, 20


def kernel(
    sizes, dil, mask_s, mask_v, pair, labels, w1, w2, gain, shift, head_t, bias_in,
    act_out, grads_out, head_out, bias_out, norm_out, loss_out,
    rowm, colm, colall, lab, hwf, hw, hw2, hb,
    pb, pf, h1, a1, h2, du, dh, yf, zb, yp, yr, zz, zt, st1, st2, st3, part, gath, red,
    halo_s, halo_r, send_s, recv_s,
):
    R, W, C, nr, nc = sizes
    n = nr * nc
    q = W // R
    group, owners = GROUP, OWNERS
    bins = head_t.shape[0]
    extent = R * nr
    row = lax.axis_index("row")
    col = lax.axis_index("col")
    me = row * nc + col
    my_owner = (me * owners + n - 1) // n
    is_owner = jnp.logical_and(my_owner < owners, (my_owner * n) // owners == me)

    def device(p):
        return (p // nc, p % nc)

    def to_all(slots):
        def step(k, carry):
            pltpu.make_async_remote_copy(
                src_ref=slots[0], dst_ref=slots[0], send_sem=slots[1], recv_sem=slots[2],
                device_id=device((me + k) % n), device_id_type=MESH,
            ).start()
            return carry

        lax.fori_loop(1, n, step, 0)

    def wait_bytes(ref, sem):
        pltpu.make_async_copy(ref, ref, sem).wait()

    def halo_copy(phase, index, src, src_at, dst, dst_at, width):
        dr, dc = DIRECTIONS[index]
        hr, hc = width

        def span(delta, edge, length, src_zero, dst_zero):
            if delta == 0:
                return pl.ds(src_zero, length), pl.ds(dst_zero, length)
            if delta > 0:
                return pl.ds(src_zero + length - edge, edge), pl.ds(dst_zero - edge, edge)
            return pl.ds(src_zero, edge), pl.ds(dst_zero + length, edge)

        sr, tr = span(dr, hr, R, src_at[0], dst_at[0])
        sc, tc = span(dc, hc, W, src_at[1], dst_at[1])
        return pltpu.make_async_remote_copy(
            src_ref=src.at[sr, sc, :], dst_ref=dst.at[tr, tc, :],
            send_sem=halo_s.at[phase, index], recv_sem=halo_r.at[phase, index],
            device_id=(row + dr, col + dc), device_id_type=MESH,
        )

    def inside(r, c):
        return (r >= 0) & (r < nr) & (c >= 0) & (c < nc)

    def halo_start(*spec):
        for index, (dr, dc) in enumerate(DIRECTIONS):
            @pl.when(inside(row + dr, col + dc))
            def _():
                halo_copy(spec[0], index, *spec[1:]).start()

    def halo_recv(*spec):
        for index, (dr, dc) in enumerate(DIRECTIONS):
            @pl.when(inside(row - dr, col - dc))
            def _():
                halo_copy(spec[0], index, *spec[1:]).wait_recv()

    def halo_sent(*spec):
        for index, (dr, dc) in enumerate(DIRECTIONS):
            @pl.when(inside(row + dr, col + dc))
            def _():
                halo_copy(spec[0], index, *spec[1:]).wait_send()

    def blocks(count, body):
        if count == 1:
            body(0)
        else:
            def step(k, carry):
                body(pl.multiple_of(k * 8, 8))
                return carry

            lax.fori_loop(0, count, step, 0)

    def pmask(first, lanes):
        return rowm[pl.ds(first + 4, 8), :, :lanes] * colm[8 : 8 + W, :lanes][None]

    def window(ref, r, c, cols):
        return ref[pl.ds(r, 8), pl.ds(c, cols), :].astype(BF16).reshape(8 * cols, C)

    taps = [(a, b) for a in (-1, 0, 1) for b in (-1, 0, 1)]
    barrier = pltpu.get_barrier_semaphore()

    def greet(k, carry):
        pl.semaphore_signal(barrier, inc=1, device_id=device((me + k) % n), device_id_type=MESH)
        return carry

    pb[...] = jnp.zeros_like(pb)
    h2[...] = jnp.zeros_like(h2)
    du[...] = jnp.zeros_like(du)
    lax.fori_loop(1, n, greet, 0)

    def fill_row(i, carry):
        at = row * R + i - 4
        there = (at >= 0) & (at < extent)
        value = jnp.where(there, mask_s[jnp.clip(at, 0, extent - 1)], 0).astype(F32)
        rowm[i] = jnp.full((1, LANES), value, F32)
        return carry

    lax.fori_loop(0, R + 8, fill_row, 0)
    spread = jnp.broadcast_to(mask_v[...].astype(F32), (LANES, extent)).T
    colall[0:8, :] = jnp.zeros((8, LANES), F32)
    colall[8 : 8 + extent, :] = spread
    colall[8 + extent : 16 + extent, :] = jnp.zeros((8, LANES), F32)
    colm[...] = colall[pl.ds(pl.multiple_of(col * W, 8), W + 16), :]
    valid = jnp.sum(spread, axis=0, keepdims=True)
    inv_wide = 1.0 / (valid * valid)
    inv_count = inv_wide[:, :C]
    pl.semaphore_wait(barrier, n - 1)

    pair_spec = (0, pair, (0, 0), pb, (8, 16), (8, 16))
    halo_start(*pair_spec)
    pb[8 : 8 + R, 16 : 16 + W, :] = pair[...]
    hwf[...] = jnp.zeros_like(hwf)
    hwf[0:bins, :] = head_t[...].astype(F32)
    hb[...] = jnp.full((1, LANES), -1e30, F32)
    hb[:, 0:bins] = bias_in[...]
    wide = hwf[...]
    hw[...] = wide.astype(BF16)
    none = jnp.zeros((LANES, C), F32)
    hw2[0:LANES, :] = jnp.concatenate([wide, none], axis=1).astype(BF16)
    hw2[LANES : 2 * LANES, :] = jnp.concatenate([none, wide], axis=1).astype(BF16)
    halo_recv(*pair_spec)
    pf[...] = pb[...].astype(F32)

    d0 = dil[0]
    d1 = dil[1]

    def first_conv(r):
        total = None
        for t, (a, b) in enumerate(taps):
            x = window(pf, r + 4 + a * d0, 8 + b * d0, W + 16)
            term = lax.dot_general(x, w1[t], NT, preferred_element_type=F32)
            total = term if total is None else total + term
        h1[pl.ds(r, 8)] = total.reshape(8, W + 16, C)

    blocks((R + 8) // 8, first_conv)

    def moments(ref, slots, phase):
        def body(first, r):
            h = ref[pl.ds(4 + r, 8), 8 : 8 + W, :]
            mh = pmask(r, C) * h
            s1 = jnp.sum(mh.reshape(8 * W, C), axis=0, keepdims=True)
            s2 = jnp.sum((mh * h).reshape(8 * W, C), axis=0, keepdims=True)
            value = jnp.concatenate([s1, s2], axis=1)
            slots[me] = value if first else slots[me] + value

        body(True, 0)
        if R > 8:
            lax.fori_loop(1, R // 8, lambda k, z: (body(False, pl.multiple_of(k * 8, 8)), z)[1], 0)
        to_all((slots.at[me], send_s.at[phase], recv_s.at[phase]))

    def gathered(slots, phase):
        wait_bytes(slots.at[pl.ds(0, n - 1)], recv_s.at[phase])
        return jnp.sum(slots[...], axis=0)

    def mean_inverse(sums):
        mean = sums[:, :C] * inv_count
        var = sums[:, C:] * inv_count - mean * mean
        return mean, 1.0 / jnp.sqrt(var + EPSILON)

    moments(h1, st1, 0)

    def spread_labels(r, carry):
        lab[r] = jnp.broadcast_to(labels[pl.ds(r, 1), :].astype(F32), (LANES, W)).T
        return carry

    lax.fori_loop(0, R, spread_labels, 0)
    mean1, inv1 = mean_inverse(gathered(st1, 0))
    scale1 = gain[0:1, :] * inv1
    shift1 = shift[0:1, :] - mean1 * scale1

    def first_act(r):
        v = h1[pl.ds(r, 8)] * scale1[None] + shift1[None]
        m = rowm[pl.ds(r, 8), :, :C] * colm[:, :C][None]
        a1[pl.ds(r, 8)] = (m * elu(v)).astype(BF16).astype(F32)

    blocks((R + 8) // 8, first_act)

    def second_conv(r):
        total = None
        for t, (a, b) in enumerate(taps):
            x = window(a1, r + 4 + a * d1, 8 + b * d1, W)
            term = lax.dot_general(x, w2[t], NT, preferred_element_type=F32)
            total = term if total is None else total + term
        h2[pl.ds(4 + r, 8), 8 : 8 + W, :] = total.reshape(8, W, C)

    blocks(R // 8, second_conv)
    moments(h2, st2, 1)
    h2_spec = (1, h2, (4, 8), h2, (4, 8), (4, 8))
    halo_start(*h2_spec)
    mean2, inv2 = mean_inverse(gathered(st2, 1))
    gain2 = gain[1:2, :]

    def features(r):
        xhat = (h2[pl.ds(4 + r, 8), 8 : 8 + W, :] - mean2[None]) * inv2[None]
        u = gain2[None] * xhat + shift[1:2, :][None] + pf[pl.ds(8 + r, 8), 16 : 16 + W, :]
        return xhat, u

    def head(r):
        _, u = features(r)
        yf[pl.ds(r, 8)] = (pmask(r, C) * elu(u)).astype(BF16).astype(F32)

    blocks(R // 8, head)

    half = R // 2
    has_self = row // q == col
    mine = row % q

    def mirror_copy(b):
        return pltpu.make_async_remote_copy(
            src_ref=yp.at[b], dst_ref=yr.at[mine],
            send_sem=send_s.at[2], recv_sem=recv_s.at[2],
            device_id=(col * q + b, row // q), device_id_type=MESH,
        )

    for b in range(q):
        stays = has_self & (mine == b)
        block = yf[:, b * R : (b + 1) * R, :]
        packed = jnp.concatenate([block[:half], block[half:]], axis=2)
        yp[b] = packed.reshape(half * R, LANES).astype(BF16)

        @pl.when(jnp.logical_not(stays))
        def _():
            mirror_copy(b).start()

        @pl.when(stays)
        def _():
            yr[b] = yp[b]

    def logits(r):
        y = yf[pl.ds(r, 8)].astype(BF16).reshape(8 * W, C)
        z = lax.dot_general(y, hw[...], NT, preferred_element_type=F32) + hb[...]
        zb[pl.ds(r, 8)] = z.reshape(8, W, LANES)

    blocks(R // 8, logits)

    @pl.when(has_self)
    def _():
        wait_bytes(yr.at[pl.ds(0, q - 1)], recv_s.at[2])

    @pl.when(jnp.logical_not(has_self))
    def _():
        wait_bytes(yr, recv_s.at[2])

    zz[...] = lax.dot_general(
        yr[...].reshape(q * half * R, LANES), hw2[...], NT, preferred_element_type=F32
    )
    for b in range(q):
        z = zz[b * half * R : (b + 1) * half * R, :]
        low = z[:, :LANES].reshape(half, R, LANES)
        high = z[:, LANES:].reshape(half, R, LANES)
        whole = jnp.concatenate([low, high], axis=0) + hb[...][None]
        zt[:, b * R : (b + 1) * R, :] = jnp.swapaxes(whole, 0, 1)

    def loss_part(first, r):
        s = 0.5 * (zb[pl.ds(r, 8)] + zt[pl.ds(r, 8)])
        top = jnp.max(s, axis=2, keepdims=True)
        log_total = top + jnp.log(jnp.sum(jnp.exp(s - top), axis=2, keepdims=True))
        bin_of = lax.broadcasted_iota(jnp.int32, (8, W, LANES), 2).astype(F32)
        hot = bin_of == lab[pl.ds(r, 8)]
        m = pmask(r, LANES)
        lossy = m * jnp.where(hot, log_total - s, 0.0)
        g = m * (jnp.exp(s - log_total) - jnp.where(hot, 1.0, 0.0))
        gh = g.astype(BF16).reshape(8 * W, LANES)
        y = yf[pl.ds(r, 8)].reshape(8 * W, C)
        head_part = jnp.dot(y.T.astype(BF16), gh, preferred_element_type=F32)
        dy = jnp.dot(gh, hw[...], preferred_element_type=F32).reshape(8, W, C)
        xhat, u = features(r)
        grad = dy * pmask(r, C) * jnp.where(u > 0, 1.0, jnp.exp(jnp.minimum(u, 0.0)))
        du[pl.ds(4 + r, 8), 8 : 8 + W, :] = grad
        s1 = jnp.sum((grad * xhat).reshape(8 * W, C), axis=0, keepdims=True)
        s2 = jnp.sum(grad.reshape(8 * W, C), axis=0, keepdims=True)
        bias = jnp.sum(g.reshape(8 * W, LANES), axis=0, keepdims=True)
        loss = jnp.sum(lossy.reshape(8 * W, LANES), axis=0, keepdims=True)
        value = jnp.concatenate(
            [jnp.concatenate([s1, s2], axis=1), bias, loss, jnp.zeros_like(loss)], axis=0
        )
        last = jnp.concatenate([jnp.zeros((C, C), F32), head_part[:, :C]], axis=1)
        last = last.reshape(8, 8, LANES)
        if first:
            st3[me] = value
            part[32:40] = last
        else:
            st3[me] = st3[me] + value
            part[32:40] = part[32:40] + last

    loss_part(True, 0)
    if R > 8:
        lax.fori_loop(
            1, R // 8, lambda k, z: (loss_part(False, pl.multiple_of(k * 8, 8)), z)[1], 0
        )
    to_all((st3.at[me], send_s.at[3], recv_s.at[3]))
    du_spec = (2, du, (4, 8), du, (4, 8), (4, 8))
    halo_start(*du_spec)
    halo_recv(*h2_spec)
    halo_recv(*du_spec)
    sums3 = gathered(st3, 3)
    bias_out[...] = sums3[1:2, :bins] / extent
    norm_out[0:1, :] = sums3[0:1, :C] / extent
    norm_out[1:2, :] = sums3[0:1, C:] / extent
    loss_out[...] = jnp.sum(sums3[2:3, :], axis=1, keepdims=True) * inv_wide[:, 0:1]
    scale_mean = sums3[0:1, :C] * inv_count
    shift_mean = sums3[0:1, C:] * inv_count
    back = gain2 * inv2

    def second_grad(r):
        m = rowm[pl.ds(r, 8), :, :C] * colm[:, :C][None]
        xhat = (h2[pl.ds(r, 8)] - mean2[None]) * inv2[None]
        v = m * back[None] * (du[pl.ds(r, 8)] - shift_mean[None] - xhat * scale_mean[None])
        dh[pl.ds(r, 8)] = v.astype(BF16).astype(F32)

    blocks((R + 8) // 8, second_grad)

    def weight_grad(first, r):
        d = dh[pl.ds(4 + r, 8), 8 : 8 + W, :].reshape(8 * W, C)
        dt = d.T.astype(BF16)
        terms = []
        for a, b in taps:
            x = window(a1, r + 4 + a * d1, 8 + b * d1, W)
            terms.append(jnp.dot(dt, x, preferred_element_type=F32))
        terms.append(jnp.zeros((C, C), F32))
        for k in range(5):
            value = jnp.concatenate(terms[2 * k : 2 * k + 2], axis=1).reshape(8, 8, LANES)
            if first and k < 4:
                part[8 * k : 8 * k + 8] = value
            else:
                part[8 * k : 8 * k + 8] = part[8 * k : 8 * k + 8] + value

    weight_grad(True, 0)
    if R > 8:
        lax.fori_loop(
            1, R // 8, lambda k, z: (weight_grad(False, pl.multiple_of(k * 8, 8)), z)[1], 0
        )

    def scatter(k, carry):
        target = (k * n) // owners

        @pl.when(target != me)
        def _():
            pltpu.make_async_remote_copy(
                src_ref=part.at[pl.ds(k * group, group)], dst_ref=gath.at[me],
                send_sem=send_s.at[4], recv_sem=recv_s.at[4],
                device_id=device(target), device_id_type=MESH,
            ).start()

        @pl.when(target == me)
        def _():
            gath[me] = part[pl.ds(k * group, group)]

        return carry

    lax.fori_loop(0, owners, scatter, 0)

    def input_grad(r):
        total = None
        for t, (a, b) in enumerate(taps):
            x = window(dh, r + 4 - a * d1, 8 - b * d1, W)
            term = jnp.dot(x, w2[t], preferred_element_type=F32)
            total = term if total is None else total + term
        act_out[pl.ds(r, 8)] = total.reshape(8, W, C).astype(BF16)

    blocks(R // 8, input_grad)

    @pl.when(is_owner)
    def _():
        wait_bytes(gath.at[pl.ds(0, n - 1)], recv_s.at[4])
        total = jnp.sum(gath[...], axis=0).reshape(8 * group, LANES)
        red[my_owner] = total.astype(BF16)
        to_all((red.at[my_owner], send_s.at[5], recv_s.at[5]))
        wait_bytes(red.at[pl.ds(0, owners - 1)], recv_s.at[5])

    @pl.when(jnp.logical_not(is_owner))
    def _():
        wait_bytes(red, recv_s.at[5])

    sums = red[...].astype(F32) * (1.0 / extent)
    for k in range(5):
        pair_of = sums[4 * k : 4 * k + 4].reshape(C, LANES)
        grads_out[2 * k] = pair_of[:, :C]
        if k < 4:
            grads_out[2 * k + 1] = pair_of[:, C:]
        else:
            head_out[...] = pair_of[:, C:].T[:bins, :]

    halo_sent(*pair_spec)
    halo_sent(*h2_spec)
    halo_sent(*du_spec)
    wait_bytes(st1.at[pl.ds(0, n - 1)], send_s.at[0])
    wait_bytes(st2.at[pl.ds(0, n - 1)], send_s.at[1])
    wait_bytes(st3.at[pl.ds(0, n - 1)], send_s.at[3])

    @pl.when(has_self)
    def _():
        wait_bytes(yp.at[pl.ds(0, q - 1)], send_s.at[2])

    @pl.when(jnp.logical_not(has_self))
    def _():
        wait_bytes(yp, send_s.at[2])

    @pl.when(is_owner)
    def _():
        wait_bytes(part.at[pl.ds(0, (owners - 1) * group)], send_s.at[4])
        wait_bytes(gath.at[pl.ds(0, n - 1), pl.ds(0, 1)], send_s.at[5])

    @pl.when(jnp.logical_not(is_owner))
    def _():
        wait_bytes(part, send_s.at[4])


def body(
    pair, dilations, mask, labels, conv_first, conv_second,
    norm_gain, norm_shift, head_weight, head_bias,
):
    C, R, W = pair.shape
    K = head_weight.shape[1]
    nr, nc = lax.axis_size("row"), lax.axis_size("col")
    n = nr * nc
    vmem = pl.BlockSpec(memory_space=pltpu.VMEM)
    smem = pl.BlockSpec(memory_space=pltpu.SMEM)
    ring = (R + 8, W + 16, C)
    act, grads, head, bias, norm, loss = pl.pallas_call(
        functools.partial(kernel, (R, W, C, nr, nc)),
        out_shape=(
            jax.ShapeDtypeStruct((R, W, C), BF16),
            jax.ShapeDtypeStruct((9, C, C), F32),
            jax.ShapeDtypeStruct((K, C), F32),
            jax.ShapeDtypeStruct((1, K), F32),
            jax.ShapeDtypeStruct((2, C), F32),
            jax.ShapeDtypeStruct((1, 1), F32),
        ),
        in_specs=[smem, smem] + [vmem] * 9,
        out_specs=(vmem,) * 6,
        scratch_shapes=[
            pltpu.VMEM((R + 8, 1, LANES), F32),
            pltpu.VMEM((W + 16, LANES), F32),
            pltpu.VMEM((R * nr + 16, LANES), F32),
            pltpu.VMEM((R, W, LANES), F32),
            pltpu.VMEM((LANES, C), F32),
            pltpu.VMEM((LANES, C), BF16),
            pltpu.VMEM((2 * LANES, LANES), BF16),
            pltpu.VMEM((1, LANES), F32),
            pltpu.VMEM((R + 16, W + 32, C), BF16),
            pltpu.VMEM((R + 16, W + 32, C), F32),
            pltpu.VMEM(ring, F32),
            pltpu.VMEM(ring, F32),
            pltpu.VMEM(ring, F32),
            pltpu.VMEM(ring, F32),
            pltpu.VMEM(ring, F32),
            pltpu.VMEM((R, W, C), F32),
            pltpu.VMEM((R, W, LANES), F32),
            pltpu.VMEM((W // R, R * R // 2, LANES), BF16),
            pltpu.VMEM((W // R, R * R // 2, LANES), BF16),
            pltpu.VMEM((W * R // 2, 2 * LANES), F32),
            pltpu.VMEM((R, W, LANES), F32),
            pltpu.VMEM((n, 1, LANES), F32),
            pltpu.VMEM((n, 1, LANES), F32),
            pltpu.VMEM((n, 4, LANES), F32),
            pltpu.VMEM((40, 8, LANES), F32),
            pltpu.VMEM((n, GROUP, 8, LANES), F32),
            pltpu.VMEM((OWNERS, 8 * GROUP, LANES), BF16),
            pltpu.SemaphoreType.DMA((3, 8)),
            pltpu.SemaphoreType.DMA((3, 8)),
            pltpu.SemaphoreType.DMA((6,)),
            pltpu.SemaphoreType.DMA((6,)),
        ],
        compiler_params=pltpu.CompilerParams(
            collective_id=0, has_side_effects=True, vmem_limit_bytes=56 * 1024 * 1024
        ),
    )(
        dilations, mask, mask[None], pair.transpose(1, 2, 0), labels,
        conv_first, conv_second, norm_gain, norm_shift, head_weight.T, head_bias[None],
    )
    return loss[0, 0], head.T, bias[0], norm, grads, act.transpose(2, 0, 1)


def solution(mesh):
    placed = (P(None, "row", "col"), P(), P(), P("row", "col"), P(), P(), P(), P(), P(), P())
    return jax.shard_map(
        body,
        mesh=mesh,
        in_specs=placed,
        out_specs=(P(), P(), P(), P(), P(), P(None, "row", "col")),
        check_vma=False,
    )
```

```python
import functools

import jax
import jax.numpy as jnp
from jax import lax
from jax.experimental import pallas as pl
from jax.experimental.pallas import tpu as pltpu
from jax.sharding import PartitionSpec as P

EPSILON = 1e-05
LANES = 128
MESH = pl.DeviceIdType.MESH
F32 = jnp.float32
BF16 = jnp.bfloat16
NT = (((1,), (1,)), ((), ()))
DIRECTIONS = tuple((a, b) for a in (-1, 0, 1) for b in (-1, 0, 1) if (a, b) != (0, 0))


def elu(v):
    return jnp.where(v > 0, v, jnp.exp(jnp.minimum(v, 0.0)) - 1.0)


GROUP, OWNERS = 2, 20


def kernel(
    sizes, dil, mask_s, mask_v, pair, labels, w1, w2, gain, shift, head_t, bias_in,
    act_out, grads_out, head_out, bias_out, norm_out, loss_out,
    rowm, colm, colall, lab, hwf, hw, hw2, hb,
    pb, pf, h1, a1, h2, du, dh, yf, zb, yp, yr, zz, zt, st1, st2, st3, part, sent, gath, red,
    halo_s, halo_r, send_s, recv_s,
):
    R, W, C, nr, nc = sizes
    n = nr * nc
    q = W // R
    group, owners = GROUP, OWNERS
    bins = head_t.shape[0]
    extent = R * nr
    row = lax.axis_index("row")
    col = lax.axis_index("col")
    me = row * nc + col
    my_owner = (me * owners + n - 1) // n
    is_owner = jnp.logical_and(my_owner < owners, (my_owner * n) // owners == me)

    def device(p):
        return (lax.div(p, nc), lax.rem(p, nc))

    def to_all(slots):
        def step(k, carry):
            pltpu.make_async_remote_copy(
                src_ref=slots[0], dst_ref=slots[0], send_sem=slots[1], recv_sem=slots[2],
                device_id=device(lax.rem(me + k, n)), device_id_type=MESH,
            ).start()
            return carry

        lax.fori_loop(1, n, step, 0, unroll=4)

    def wait_bytes(ref, sem):
        pltpu.make_async_copy(ref, ref, sem).wait()

    def halo_copy(phase, index, src, src_at, dst, dst_at, width):
        dr, dc = DIRECTIONS[index]
        hr, hc = width

        def span(delta, edge, length, src_zero, dst_zero):
            if delta == 0:
                return pl.ds(src_zero, length), pl.ds(dst_zero, length)
            if delta > 0:
                return pl.ds(src_zero + length - edge, edge), pl.ds(dst_zero - edge, edge)
            return pl.ds(src_zero, edge), pl.ds(dst_zero + length, edge)

        sr, tr = span(dr, hr, R, src_at[0], dst_at[0])
        sc, tc = span(dc, hc, W, src_at[1], dst_at[1])
        return pltpu.make_async_remote_copy(
            src_ref=src.at[sr, sc, :], dst_ref=dst.at[tr, tc, :],
            send_sem=halo_s.at[phase, index], recv_sem=halo_r.at[phase, index],
            device_id=(row + dr, col + dc), device_id_type=MESH,
        )

    def inside(r, c):
        return (r >= 0) & (r < nr) & (c >= 0) & (c < nc)

    def halo_start(*spec):
        for index, (dr, dc) in enumerate(DIRECTIONS):
            @pl.when(inside(row + dr, col + dc))
            def _():
                halo_copy(spec[0], index, *spec[1:]).start()

    def halo_recv(*spec):
        for index, (dr, dc) in enumerate(DIRECTIONS):
            @pl.when(inside(row - dr, col - dc))
            def _():
                halo_copy(spec[0], index, *spec[1:]).wait_recv()

    def halo_sent(*spec):
        for index, (dr, dc) in enumerate(DIRECTIONS):
            @pl.when(inside(row + dr, col + dc))
            def _():
                halo_copy(spec[0], index, *spec[1:]).wait_send()

    def blocks(count, body):
        if count == 1:
            body(0)
        else:
            def step(k, carry):
                body(pl.multiple_of(k * 8, 8))
                return carry

            lax.fori_loop(0, count, step, 0)

    def pmask(first, lanes):
        return rowm[pl.ds(first + 4, 8), :, :lanes] * colm[8 : 8 + W, :lanes][None]

    def window(ref, r, c, cols):
        return ref[pl.ds(r, 8), pl.ds(c, cols), :].astype(BF16).reshape(8 * cols, C)

    taps = [(a, b) for a in (-1, 0, 1) for b in (-1, 0, 1)]
    barrier = pltpu.get_barrier_semaphore()

    def greet(k, carry):
        pl.semaphore_signal(barrier, inc=1, device_id=device(lax.rem(me + k, n)), device_id_type=MESH)
        return carry

    pb[...] = jnp.zeros_like(pb)
    h2[...] = jnp.zeros_like(h2)
    du[...] = jnp.zeros_like(du)
    lax.fori_loop(1, n, greet, 0)

    def fill_row(i, carry):
        at = row * R + i - 4
        there = (at >= 0) & (at < extent)
        value = jnp.where(there, mask_s[jnp.clip(at, 0, extent - 1)], 0).astype(F32)
        rowm[i] = jnp.full((1, LANES), value, F32)
        return carry

    lax.fori_loop(0, R + 8, fill_row, 0)
    spread = jnp.broadcast_to(mask_v[...].astype(F32), (LANES, extent)).T
    colall[0:8, :] = jnp.zeros((8, LANES), F32)
    colall[8 : 8 + extent, :] = spread
    colall[8 + extent : 16 + extent, :] = jnp.zeros((8, LANES), F32)
    colm[...] = colall[pl.ds(pl.multiple_of(col * W, 8), W + 16), :]
    valid = jnp.sum(spread, axis=0, keepdims=True)
    inv_wide = 1.0 / (valid * valid)
    inv_count = inv_wide[:, :C]
    pl.semaphore_wait(barrier, n - 1)

    pair_spec = (0, pair, (0, 0), pb, (8, 16), (8, 16))
    halo_start(*pair_spec)
    pb[8 : 8 + R, 16 : 16 + W, :] = pair[...]
    hwf[...] = jnp.zeros_like(hwf)
    hwf[0:bins, :] = head_t[...].astype(F32)
    hb[...] = jnp.full((1, LANES), -1e30, F32)
    hb[:, 0:bins] = bias_in[...]
    wide = hwf[...]
    hw[...] = wide.astype(BF16)
    none = jnp.zeros((LANES, C), F32)
    hw2[0:LANES, :] = jnp.concatenate([wide, none], axis=1).astype(BF16)
    hw2[LANES : 2 * LANES, :] = jnp.concatenate([none, wide], axis=1).astype(BF16)
    halo_recv(*pair_spec)
    pf[...] = pb[...].astype(F32)

    d0 = dil[0]
    d1 = dil[1]

    def first_conv(r):
        total = None
        for t, (a, b) in enumerate(taps):
            x = window(pf, r + 4 + a * d0, 8 + b * d0, W + 16)
            term = lax.dot_general(x, w1[t], NT, preferred_element_type=F32)
            total = term if total is None else total + term
        h1[pl.ds(r, 8)] = total.reshape(8, W + 16, C)

    blocks((R + 8) // 8, first_conv)

    def moments(ref, slots, phase):
        def body(first, r):
            h = ref[pl.ds(4 + r, 8), 8 : 8 + W, :]
            mh = pmask(r, C) * h
            s1 = jnp.sum(mh.reshape(8 * W, C), axis=0, keepdims=True)
            s2 = jnp.sum((mh * h).reshape(8 * W, C), axis=0, keepdims=True)
            value = jnp.concatenate([s1, s2], axis=1)
            slots[me] = value if first else slots[me] + value

        body(True, 0)
        if R > 8:
            lax.fori_loop(1, R // 8, lambda k, z: (body(False, pl.multiple_of(k * 8, 8)), z)[1], 0)
        to_all((slots.at[me], send_s.at[phase], recv_s.at[phase]))

    def gathered(slots, phase):
        wait_bytes(slots.at[pl.ds(0, n - 1)], recv_s.at[phase])
        return jnp.sum(slots[...], axis=0)

    def mean_inverse(sums):
        mean = sums[:, :C] * inv_count
        var = sums[:, C:] * inv_count - mean * mean
        return mean, 1.0 / jnp.sqrt(var + EPSILON)

    moments(h1, st1, 0)

    def spread_labels(r, carry):
        lab[r] = jnp.broadcast_to(labels[pl.ds(r, 1), :].astype(F32), (LANES, W)).T
        return carry

    lax.fori_loop(0, R, spread_labels, 0)
    mean1, inv1 = mean_inverse(gathered(st1, 0))
    scale1 = gain[0:1, :] * inv1
    shift1 = shift[0:1, :] - mean1 * scale1

    def first_act(r):
        v = h1[pl.ds(r, 8)] * scale1[None] + shift1[None]
        m = rowm[pl.ds(r, 8), :, :C] * colm[:, :C][None]
        a1[pl.ds(r, 8)] = (m * elu(v)).astype(BF16).astype(F32)

    blocks((R + 8) // 8, first_act)

    def second_conv(r):
        total = None
        for t, (a, b) in enumerate(taps):
            x = window(a1, r + 4 + a * d1, 8 + b * d1, W)
            term = lax.dot_general(x, w2[t], NT, preferred_element_type=F32)
            total = term if total is None else total + term
        h2[pl.ds(4 + r, 8), 8 : 8 + W, :] = total.reshape(8, W, C)

    blocks(R // 8, second_conv)
    moments(h2, st2, 1)
    h2_spec = (1, h2, (4, 8), h2, (4, 8), (4, 8))
    halo_start(*h2_spec)
    mean2, inv2 = mean_inverse(gathered(st2, 1))
    gain2 = gain[1:2, :]

    def features(r):
        xhat = (h2[pl.ds(4 + r, 8), 8 : 8 + W, :] - mean2[None]) * inv2[None]
        u = gain2[None] * xhat + shift[1:2, :][None] + pf[pl.ds(8 + r, 8), 16 : 16 + W, :]
        return xhat, u

    def head(r):
        _, u = features(r)
        yf[pl.ds(r, 8)] = (pmask(r, C) * elu(u)).astype(BF16).astype(F32)

    blocks(R // 8, head)

    half = R // 2
    has_self = row // q == col
    mine = row % q

    def mirror_copy(b):
        return pltpu.make_async_remote_copy(
            src_ref=yp.at[b], dst_ref=yr.at[mine],
            send_sem=send_s.at[2], recv_sem=recv_s.at[2],
            device_id=(col * q + b, row // q), device_id_type=MESH,
        )

    for b in range(q):
        stays = has_self & (mine == b)
        block = yf[:, b * R : (b + 1) * R, :]
        packed = jnp.concatenate([block[:half], block[half:]], axis=2)
        yp[b] = packed.reshape(half * R, LANES).astype(BF16)

        @pl.when(jnp.logical_not(stays))
        def _():
            mirror_copy(b).start()

        @pl.when(stays)
        def _():
            yr[b] = yp[b]

    def logits(r):
        y = yf[pl.ds(r, 8)].astype(BF16).reshape(8 * W, C)
        z = lax.dot_general(y, hw[...], NT, preferred_element_type=F32) + hb[...]
        zb[pl.ds(r, 8)] = z.reshape(8, W, LANES)

    blocks(R // 8, logits)

    @pl.when(has_self)
    def _():
        wait_bytes(yr.at[pl.ds(0, q - 1)], recv_s.at[2])

    @pl.when(jnp.logical_not(has_self))
    def _():
        wait_bytes(yr, recv_s.at[2])

    zz[...] = lax.dot_general(
        yr[...].reshape(q * half * R, LANES), hw2[...], NT, preferred_element_type=F32
    )
    for b in range(q):
        z = zz[b * half * R : (b + 1) * half * R, :]
        low = z[:, :LANES].reshape(half, R, LANES)
        high = z[:, LANES:].reshape(half, R, LANES)
        whole = jnp.concatenate([low, high], axis=0) + hb[...][None]
        zt[:, b * R : (b + 1) * R, :] = jnp.swapaxes(whole, 0, 1)

    def loss_part(first, r):
        s = 0.5 * (zb[pl.ds(r, 8)] + zt[pl.ds(r, 8)])
        top = jnp.max(s, axis=2, keepdims=True)
        log_total = top + jnp.log(jnp.sum(jnp.exp(s - top), axis=2, keepdims=True))
        bin_of = lax.broadcasted_iota(jnp.int32, (8, W, LANES), 2).astype(F32)
        hot = bin_of == lab[pl.ds(r, 8)]
        m = pmask(r, LANES)
        lossy = m * jnp.where(hot, log_total - s, 0.0)
        g = m * (jnp.exp(s - log_total) - jnp.where(hot, 1.0, 0.0))
        gh = g.astype(BF16).reshape(8 * W, LANES)
        y = yf[pl.ds(r, 8)].reshape(8 * W, C)
        head_part = jnp.dot(y.T.astype(BF16), gh, preferred_element_type=F32)
        dy = jnp.dot(gh, hw[...], preferred_element_type=F32).reshape(8, W, C)
        xhat, u = features(r)
        grad = dy * pmask(r, C) * jnp.where(u > 0, 1.0, jnp.exp(jnp.minimum(u, 0.0)))
        du[pl.ds(4 + r, 8), 8 : 8 + W, :] = grad
        s1 = jnp.sum((grad * xhat).reshape(8 * W, C), axis=0, keepdims=True)
        s2 = jnp.sum(grad.reshape(8 * W, C), axis=0, keepdims=True)
        bias = jnp.sum(g.reshape(8 * W, LANES), axis=0, keepdims=True)
        loss = jnp.sum(lossy.reshape(8 * W, LANES), axis=0, keepdims=True)
        value = jnp.concatenate(
            [jnp.concatenate([s1, s2], axis=1), bias, loss, jnp.zeros_like(loss)], axis=0
        )
        last = jnp.concatenate([jnp.zeros((C, C), F32), head_part[:, :C]], axis=1)
        last = last.reshape(8, 8, LANES)
        if first:
            st3[me] = value
            part[32:40] = last
        else:
            st3[me] = st3[me] + value
            part[32:40] = part[32:40] + last

    loss_part(True, 0)
    if R > 8:
        lax.fori_loop(
            1, R // 8, lambda k, z: (loss_part(False, pl.multiple_of(k * 8, 8)), z)[1], 0
        )
    to_all((st3.at[me], send_s.at[3], recv_s.at[3]))
    du_spec = (2, du, (4, 8), du, (4, 8), (4, 8))
    halo_start(*du_spec)
    halo_recv(*h2_spec)
    halo_recv(*du_spec)
    sums3 = gathered(st3, 3)
    bias_out[...] = sums3[1:2, :bins] / extent
    norm_out[0:1, :] = sums3[0:1, :C] / extent
    norm_out[1:2, :] = sums3[0:1, C:] / extent
    loss_out[...] = jnp.sum(sums3[2:3, :], axis=1, keepdims=True) * inv_wide[:, 0:1]
    scale_mean = sums3[0:1, :C] * inv_count
    shift_mean = sums3[0:1, C:] * inv_count
    back = gain2 * inv2

    def second_grad(r):
        m = rowm[pl.ds(r, 8), :, :C] * colm[:, :C][None]
        xhat = (h2[pl.ds(r, 8)] - mean2[None]) * inv2[None]
        v = m * back[None] * (du[pl.ds(r, 8)] - shift_mean[None] - xhat * scale_mean[None])
        dh[pl.ds(r, 8)] = v.astype(BF16).astype(F32)

    blocks((R + 8) // 8, second_grad)

    def weight_grad(first, r):
        d = dh[pl.ds(4 + r, 8), 8 : 8 + W, :].reshape(8 * W, C)
        dt = d.T.astype(BF16)
        terms = []
        for a, b in taps:
            x = window(a1, r + 4 + a * d1, 8 + b * d1, W)
            terms.append(jnp.dot(dt, x, preferred_element_type=F32))
        terms.append(jnp.zeros((C, C), F32))
        for k in range(5):
            value = jnp.concatenate(terms[2 * k : 2 * k + 2], axis=1).reshape(8, 8, LANES)
            if first and k < 4:
                part[8 * k : 8 * k + 8] = value
            else:
                part[8 * k : 8 * k + 8] = part[8 * k : 8 * k + 8] + value

    weight_grad(True, 0)
    if R > 8:
        lax.fori_loop(
            1, R // 8, lambda k, z: (weight_grad(False, pl.multiple_of(k * 8, 8)), z)[1], 0
        )

    sent[...] = part[...].reshape(owners, 8 * group, LANES).astype(BF16)

    def scatter(k, carry):
        target = lax.div(k * n, owners)

        @pl.when(target != me)
        def _():
            pltpu.make_async_remote_copy(
                src_ref=sent.at[k], dst_ref=gath.at[me],
                send_sem=send_s.at[4], recv_sem=recv_s.at[4],
                device_id=device(target), device_id_type=MESH,
            ).start()

        @pl.when(target == me)
        def _():
            gath[me] = sent[k]

        return carry

    lax.fori_loop(0, owners, scatter, 0)

    def input_grad(r):
        total = None
        for t, (a, b) in enumerate(taps):
            x = window(dh, r + 4 - a * d1, 8 - b * d1, W)
            term = jnp.dot(x, w2[t], preferred_element_type=F32)
            total = term if total is None else total + term
        act_out[pl.ds(r, 8)] = total.reshape(8, W, C).astype(BF16)

    blocks(R // 8, input_grad)

    @pl.when(is_owner)
    def _():
        wait_bytes(gath.at[pl.ds(0, n - 1)], recv_s.at[4])
        total = jnp.sum(gath[...].astype(F32), axis=0)
        red[my_owner] = total.astype(BF16)
        to_all((red.at[my_owner], send_s.at[5], recv_s.at[5]))
        wait_bytes(red.at[pl.ds(0, owners - 1)], recv_s.at[5])

    @pl.when(jnp.logical_not(is_owner))
    def _():
        wait_bytes(red, recv_s.at[5])

    sums = red[...].astype(F32) * (1.0 / extent)
    grads_out[...] = sums.reshape(5, C, LANES)
    head_out[...] = sums[16:20].reshape(C, LANES)[:, C:].T[:bins, :]

    halo_sent(*pair_spec)
    halo_sent(*h2_spec)
    halo_sent(*du_spec)
    wait_bytes(st1.at[pl.ds(0, n - 1)], send_s.at[0])
    wait_bytes(st2.at[pl.ds(0, n - 1)], send_s.at[1])
    wait_bytes(st3.at[pl.ds(0, n - 1)], send_s.at[3])

    @pl.when(has_self)
    def _():
        wait_bytes(yp.at[pl.ds(0, q - 1)], send_s.at[2])

    @pl.when(jnp.logical_not(has_self))
    def _():
        wait_bytes(yp, send_s.at[2])

    @pl.when(is_owner)
    def _():
        wait_bytes(sent.at[pl.ds(0, owners - 1)], send_s.at[4])
        wait_bytes(gath.at[pl.ds(0, n - 1)], send_s.at[5])

    @pl.when(jnp.logical_not(is_owner))
    def _():
        wait_bytes(sent, send_s.at[4])


def body(
    pair, dilations, mask, labels, conv_first, conv_second,
    norm_gain, norm_shift, head_weight, head_bias,
):
    C, R, W = pair.shape
    K = head_weight.shape[1]
    nr, nc = lax.axis_size("row"), lax.axis_size("col")
    n = nr * nc
    vmem = pl.BlockSpec(memory_space=pltpu.VMEM)
    smem = pl.BlockSpec(memory_space=pltpu.SMEM)
    ring = (R + 8, W + 16, C)
    act, grads, head, bias, norm, loss = pl.pallas_call(
        functools.partial(kernel, (R, W, C, nr, nc)),
        out_shape=(
            jax.ShapeDtypeStruct((R, W, C), BF16),
            jax.ShapeDtypeStruct((5, C, LANES), F32),
            jax.ShapeDtypeStruct((K, C), F32),
            jax.ShapeDtypeStruct((1, K), F32),
            jax.ShapeDtypeStruct((2, C), F32),
            jax.ShapeDtypeStruct((1, 1), F32),
        ),
        in_specs=[smem, smem] + [vmem] * 9,
        out_specs=(vmem,) * 6,
        scratch_shapes=[
            pltpu.VMEM((R + 8, 1, LANES), F32),
            pltpu.VMEM((W + 16, LANES), F32),
            pltpu.VMEM((R * nr + 16, LANES), F32),
            pltpu.VMEM((R, W, LANES), F32),
            pltpu.VMEM((LANES, C), F32),
            pltpu.VMEM((LANES, C), BF16),
            pltpu.VMEM((2 * LANES, LANES), BF16),
            pltpu.VMEM((1, LANES), F32),
            pltpu.VMEM((R + 16, W + 32, C), BF16),
            pltpu.VMEM((R + 16, W + 32, C), F32),
            pltpu.VMEM(ring, F32),
            pltpu.VMEM(ring, F32),
            pltpu.VMEM(ring, F32),
            pltpu.VMEM(ring, F32),
            pltpu.VMEM(ring, F32),
            pltpu.VMEM((R, W, C), F32),
            pltpu.VMEM((R, W, LANES), F32),
            pltpu.VMEM((W // R, R * R // 2, LANES), BF16),
            pltpu.VMEM((W // R, R * R // 2, LANES), BF16),
            pltpu.VMEM((W * R // 2, 2 * LANES), F32),
            pltpu.VMEM((R, W, LANES), F32),
            pltpu.VMEM((n, 1, LANES), F32),
            pltpu.VMEM((n, 1, LANES), F32),
            pltpu.VMEM((n, 4, LANES), F32),
            pltpu.VMEM((40, 8, LANES), F32),
            pltpu.VMEM((OWNERS, 8 * GROUP, LANES), BF16),
            pltpu.VMEM((n, 8 * GROUP, LANES), BF16),
            pltpu.VMEM((OWNERS, 8 * GROUP, LANES), BF16),
            pltpu.SemaphoreType.DMA((3, 8)),
            pltpu.SemaphoreType.DMA((3, 8)),
            pltpu.SemaphoreType.DMA((6,)),
            pltpu.SemaphoreType.DMA((6,)),
        ],
        compiler_params=pltpu.CompilerParams(
            collective_id=0, has_side_effects=True, vmem_limit_bytes=56 * 1024 * 1024
        ),
    )(
        dilations, mask, mask[None], pair.transpose(1, 2, 0), labels,
        conv_first, conv_second, norm_gain, norm_shift, head_weight.T, head_bias[None],
    )
    grads = grads.reshape(5, C, 2, C).transpose(0, 2, 1, 3).reshape(10, C, C)[:9]
    return loss[0, 0], head.T, bias[0], norm, grads, act.transpose(2, 0, 1)


def solution(mesh):
    placed = (P(None, "row", "col"), P(), P(), P("row", "col"), P(), P(), P(), P(), P(), P())
    return jax.shard_map(
        body,
        mesh=mesh,
        in_specs=placed,
        out_specs=(P(), P(), P(), P(), P(), P(None, "row", "col")),
        check_vma=False,
    )
```

```python
import functools

import jax
import jax.numpy as jnp
from jax import lax
from jax.experimental import pallas as pl
from jax.experimental.pallas import tpu as pltpu
from jax.sharding import PartitionSpec as P

EPSILON = 1e-05
LANES = 128
MESH = pl.DeviceIdType.MESH
F32 = jnp.float32
BF16 = jnp.bfloat16
NT = (((1,), (1,)), ((), ()))
DIRECTIONS = tuple((a, b) for a in (-1, 0, 1) for b in (-1, 0, 1) if (a, b) != (0, 0))


def elu(v):
    return jnp.where(v > 0, v, jnp.exp(jnp.minimum(v, 0.0)) - 1.0)


GROUP, OWNERS = 2, 20


def kernel(
    sizes, dil, mask_s, mask_v, pair_in, labels, w1, w2, gain, shift, head_t, bias_in,
    act_out, grads_out, head_out, bias_out, norm_out, loss_out,
    pair, turned, ga, rowm, colm, colall, lab, hwf, hw, hw2, hb,
    pb, pf, h1, a1, h2, du, dh, yf, zb, yp, yr, zz, zt, st1, st2, st3, part, sent, gath, red,
    halo_s, halo_r, send_s, recv_s,
):
    R, W, C, nr, nc = sizes
    n = nr * nc
    q = W // R
    group, owners = GROUP, OWNERS
    bins = head_t.shape[0]
    extent = R * nr
    row = lax.axis_index("row")
    col = lax.axis_index("col")
    me = row * nc + col
    my_owner = (me * owners + n - 1) // n
    is_owner = jnp.logical_and(my_owner < owners, (my_owner * n) // owners == me)

    def device(p):
        return (lax.div(p, nc), lax.rem(p, nc))

    def to_all(slots):
        def step(k, carry):
            pltpu.make_async_remote_copy(
                src_ref=slots[0], dst_ref=slots[0], send_sem=slots[1], recv_sem=slots[2],
                device_id=device(lax.rem(me + k, n)), device_id_type=MESH,
            ).start()
            return carry

        lax.fori_loop(1, n, step, 0, unroll=4)

    def wait_bytes(ref, sem):
        pltpu.make_async_copy(ref, ref, sem).wait()

    def halo_copy(phase, index, src, src_at, dst, dst_at, width):
        dr, dc = DIRECTIONS[index]
        hr, hc = width

        def span(delta, edge, length, src_zero, dst_zero):
            if delta == 0:
                return pl.ds(src_zero, length), pl.ds(dst_zero, length)
            if delta > 0:
                return pl.ds(src_zero + length - edge, edge), pl.ds(dst_zero - edge, edge)
            return pl.ds(src_zero, edge), pl.ds(dst_zero + length, edge)

        sr, tr = span(dr, hr, R, src_at[0], dst_at[0])
        sc, tc = span(dc, hc, W, src_at[1], dst_at[1])
        return pltpu.make_async_remote_copy(
            src_ref=src.at[sr, sc, :], dst_ref=dst.at[tr, tc, :],
            send_sem=halo_s.at[phase, index], recv_sem=halo_r.at[phase, index],
            device_id=(row + dr, col + dc), device_id_type=MESH,
        )

    def inside(r, c):
        return (r >= 0) & (r < nr) & (c >= 0) & (c < nc)

    def halo_start(*spec):
        for index, (dr, dc) in enumerate(DIRECTIONS):
            @pl.when(inside(row + dr, col + dc))
            def _():
                halo_copy(spec[0], index, *spec[1:]).start()

    def halo_recv(*spec):
        for index, (dr, dc) in enumerate(DIRECTIONS):
            @pl.when(inside(row - dr, col - dc))
            def _():
                halo_copy(spec[0], index, *spec[1:]).wait_recv()

    def halo_sent(*spec):
        for index, (dr, dc) in enumerate(DIRECTIONS):
            @pl.when(inside(row + dr, col + dc))
            def _():
                halo_copy(spec[0], index, *spec[1:]).wait_send()

    def blocks(count, body):
        if count == 1:
            body(0)
        else:
            def step(k, carry):
                body(pl.multiple_of(k * 8, 8))
                return carry

            lax.fori_loop(0, count, step, 0)

    def pmask(first, lanes):
        return rowm[pl.ds(first + 4, 8), :, :lanes] * colm[8 : 8 + W, :lanes][None]

    def window(ref, r, c, cols):
        return ref[pl.ds(r, 8), pl.ds(c, cols), :].astype(BF16).reshape(8 * cols, C)

    taps = [(a, b) for a in (-1, 0, 1) for b in (-1, 0, 1)]
    barrier = pltpu.get_barrier_semaphore()

    def greet(k, carry):
        pl.semaphore_signal(barrier, inc=1, device_id=device(lax.rem(me + k, n)), device_id_type=MESH)
        return carry

    pb[...] = jnp.zeros_like(pb)
    h2[...] = jnp.zeros_like(h2)
    du[...] = jnp.zeros_like(du)
    lax.fori_loop(1, n, greet, 0)

    turned[...] = pair_in[...].astype(F32)
    for r in range(R):
        pair[r] = turned[:, r, :].T.astype(BF16)

    def fill_row(i, carry):
        at = row * R + i - 4
        there = (at >= 0) & (at < extent)
        value = jnp.where(there, mask_s[jnp.clip(at, 0, extent - 1)], 0).astype(F32)
        rowm[i] = jnp.full((1, LANES), value, F32)
        return carry

    lax.fori_loop(0, R + 8, fill_row, 0)
    spread = jnp.broadcast_to(mask_v[...].astype(F32), (LANES, extent)).T
    colall[0:8, :] = jnp.zeros((8, LANES), F32)
    colall[8 : 8 + extent, :] = spread
    colall[8 + extent : 16 + extent, :] = jnp.zeros((8, LANES), F32)
    colm[...] = colall[pl.ds(pl.multiple_of(col * W, 8), W + 16), :]
    valid = jnp.sum(spread, axis=0, keepdims=True)
    inv_wide = 1.0 / (valid * valid)
    inv_count = inv_wide[:, :C]
    pl.semaphore_wait(barrier, n - 1)

    pair_spec = (0, pair, (0, 0), pb, (8, 16), (8, 16))
    halo_start(*pair_spec)
    pb[8 : 8 + R, 16 : 16 + W, :] = pair[...]
    hwf[...] = jnp.zeros_like(hwf)
    hwf[0:bins, :] = head_t[...].astype(F32)
    hb[...] = jnp.full((1, LANES), -1e30, F32)
    hb[:, 0:bins] = bias_in[...]
    wide = hwf[...]
    hw[...] = wide.astype(BF16)
    none = jnp.zeros((LANES, C), F32)
    hw2[0:LANES, :] = jnp.concatenate([wide, none], axis=1).astype(BF16)
    hw2[LANES : 2 * LANES, :] = jnp.concatenate([none, wide], axis=1).astype(BF16)
    halo_recv(*pair_spec)
    pf[...] = pb[...].astype(F32)

    d0 = dil[0]
    d1 = dil[1]

    def first_conv(r):
        total = None
        for t, (a, b) in enumerate(taps):
            x = window(pf, r + 4 + a * d0, 8 + b * d0, W + 16)
            term = lax.dot_general(x, w1[t], NT, preferred_element_type=F32)
            total = term if total is None else total + term
        h1[pl.ds(r, 8)] = total.reshape(8, W + 16, C)

    blocks((R + 8) // 8, first_conv)

    def moments(ref, slots, phase):
        def body(first, r):
            h = ref[pl.ds(4 + r, 8), 8 : 8 + W, :]
            mh = pmask(r, C) * h
            s1 = jnp.sum(mh.reshape(8 * W, C), axis=0, keepdims=True)
            s2 = jnp.sum((mh * h).reshape(8 * W, C), axis=0, keepdims=True)
            value = jnp.concatenate([s1, s2], axis=1)
            slots[me] = value if first else slots[me] + value

        body(True, 0)
        if R > 8:
            lax.fori_loop(1, R // 8, lambda k, z: (body(False, pl.multiple_of(k * 8, 8)), z)[1], 0)
        to_all((slots.at[me], send_s.at[phase], recv_s.at[phase]))

    def gathered(slots, phase):
        wait_bytes(slots.at[pl.ds(0, n - 1)], recv_s.at[phase])
        return jnp.sum(slots[...], axis=0)

    def mean_inverse(sums):
        mean = sums[:, :C] * inv_count
        var = sums[:, C:] * inv_count - mean * mean
        return mean, 1.0 / jnp.sqrt(var + EPSILON)

    moments(h1, st1, 0)

    def spread_labels(r, carry):
        lab[r] = jnp.broadcast_to(labels[pl.ds(r, 1), :].astype(F32), (LANES, W)).T
        return carry

    lax.fori_loop(0, R, spread_labels, 0)
    mean1, inv1 = mean_inverse(gathered(st1, 0))
    scale1 = gain[0:1, :] * inv1
    shift1 = shift[0:1, :] - mean1 * scale1

    def first_act(r):
        v = h1[pl.ds(r, 8)] * scale1[None] + shift1[None]
        m = rowm[pl.ds(r, 8), :, :C] * colm[:, :C][None]
        a1[pl.ds(r, 8)] = (m * elu(v)).astype(BF16).astype(F32)

    blocks((R + 8) // 8, first_act)

    def second_conv(r):
        total = None
        for t, (a, b) in enumerate(taps):
            x = window(a1, r + 4 + a * d1, 8 + b * d1, W)
            term = lax.dot_general(x, w2[t], NT, preferred_element_type=F32)
            total = term if total is None else total + term
        h2[pl.ds(4 + r, 8), 8 : 8 + W, :] = total.reshape(8, W, C)

    blocks(R // 8, second_conv)
    moments(h2, st2, 1)
    h2_spec = (1, h2, (4, 8), h2, (4, 8), (4, 8))
    halo_start(*h2_spec)
    mean2, inv2 = mean_inverse(gathered(st2, 1))
    gain2 = gain[1:2, :]

    def features(r):
        xhat = (h2[pl.ds(4 + r, 8), 8 : 8 + W, :] - mean2[None]) * inv2[None]
        u = gain2[None] * xhat + shift[1:2, :][None] + pf[pl.ds(8 + r, 8), 16 : 16 + W, :]
        return xhat, u

    def head(r):
        _, u = features(r)
        yf[pl.ds(r, 8)] = (pmask(r, C) * elu(u)).astype(BF16).astype(F32)

    blocks(R // 8, head)

    half = R // 2
    has_self = row // q == col
    mine = row % q

    def mirror_copy(b):
        return pltpu.make_async_remote_copy(
            src_ref=yp.at[b], dst_ref=yr.at[mine],
            send_sem=send_s.at[2], recv_sem=recv_s.at[2],
            device_id=(col * q + b, row // q), device_id_type=MESH,
        )

    for b in range(q):
        stays = has_self & (mine == b)
        block = yf[:, b * R : (b + 1) * R, :]
        packed = jnp.concatenate([block[:half], block[half:]], axis=2)
        yp[b] = packed.reshape(half * R, LANES).astype(BF16)

        @pl.when(jnp.logical_not(stays))
        def _():
            mirror_copy(b).start()

        @pl.when(stays)
        def _():
            yr[b] = yp[b]

    def logits(r):
        y = yf[pl.ds(r, 8)].astype(BF16).reshape(8 * W, C)
        z = lax.dot_general(y, hw[...], NT, preferred_element_type=F32) + hb[...]
        zb[pl.ds(r, 8)] = z.reshape(8, W, LANES)

    blocks(R // 8, logits)

    @pl.when(has_self)
    def _():
        wait_bytes(yr.at[pl.ds(0, q - 1)], recv_s.at[2])

    @pl.when(jnp.logical_not(has_self))
    def _():
        wait_bytes(yr, recv_s.at[2])

    zz[...] = lax.dot_general(
        yr[...].reshape(q * half * R, LANES), hw2[...], NT, preferred_element_type=F32
    )
    for b in range(q):
        z = zz[b * half * R : (b + 1) * half * R, :]
        low = z[:, :LANES].reshape(half, R, LANES)
        high = z[:, LANES:].reshape(half, R, LANES)
        whole = jnp.concatenate([low, high], axis=0) + hb[...][None]
        zt[:, b * R : (b + 1) * R, :] = jnp.swapaxes(whole, 0, 1)

    def loss_part(first, r):
        s = 0.5 * (zb[pl.ds(r, 8)] + zt[pl.ds(r, 8)])
        top = jnp.max(s, axis=2, keepdims=True)
        log_total = top + jnp.log(jnp.sum(jnp.exp(s - top), axis=2, keepdims=True))
        bin_of = lax.broadcasted_iota(jnp.int32, (8, W, LANES), 2).astype(F32)
        hot = bin_of == lab[pl.ds(r, 8)]
        m = pmask(r, LANES)
        lossy = m * jnp.where(hot, log_total - s, 0.0)
        g = m * (jnp.exp(s - log_total) - jnp.where(hot, 1.0, 0.0))
        gh = g.astype(BF16).reshape(8 * W, LANES)
        y = yf[pl.ds(r, 8)].reshape(8 * W, C)
        head_part = jnp.dot(y.T.astype(BF16), gh, preferred_element_type=F32)
        dy = jnp.dot(gh, hw[...], preferred_element_type=F32).reshape(8, W, C)
        xhat, u = features(r)
        grad = dy * pmask(r, C) * jnp.where(u > 0, 1.0, jnp.exp(jnp.minimum(u, 0.0)))
        du[pl.ds(4 + r, 8), 8 : 8 + W, :] = grad
        s1 = jnp.sum((grad * xhat).reshape(8 * W, C), axis=0, keepdims=True)
        s2 = jnp.sum(grad.reshape(8 * W, C), axis=0, keepdims=True)
        bias = jnp.sum(g.reshape(8 * W, LANES), axis=0, keepdims=True)
        loss = jnp.sum(lossy.reshape(8 * W, LANES), axis=0, keepdims=True)
        value = jnp.concatenate(
            [jnp.concatenate([s1, s2], axis=1), bias, loss, jnp.zeros_like(loss)], axis=0
        )
        last = jnp.concatenate([jnp.zeros((C, C), F32), head_part[:, :C]], axis=1)
        last = last.reshape(8, 8, LANES)
        if first:
            st3[me] = value
            part[32:40] = last
        else:
            st3[me] = st3[me] + value
            part[32:40] = part[32:40] + last

    loss_part(True, 0)
    if R > 8:
        lax.fori_loop(
            1, R // 8, lambda k, z: (loss_part(False, pl.multiple_of(k * 8, 8)), z)[1], 0
        )
    to_all((st3.at[me], send_s.at[3], recv_s.at[3]))
    du_spec = (2, du, (4, 8), du, (4, 8), (4, 8))
    halo_start(*du_spec)
    halo_recv(*h2_spec)
    halo_recv(*du_spec)
    sums3 = gathered(st3, 3)
    bias_out[...] = sums3[1:2, :bins] / extent
    norm_out[0:1, :] = sums3[0:1, :C] / extent
    norm_out[1:2, :] = sums3[0:1, C:] / extent
    loss_out[...] = jnp.sum(sums3[2:3, :], axis=1, keepdims=True) * inv_wide[:, 0:1]
    scale_mean = sums3[0:1, :C] * inv_count
    shift_mean = sums3[0:1, C:] * inv_count
    back = gain2 * inv2

    def second_grad(r):
        m = rowm[pl.ds(r, 8), :, :C] * colm[:, :C][None]
        xhat = (h2[pl.ds(r, 8)] - mean2[None]) * inv2[None]
        v = m * back[None] * (du[pl.ds(r, 8)] - shift_mean[None] - xhat * scale_mean[None])
        dh[pl.ds(r, 8)] = v.astype(BF16).astype(F32)

    blocks((R + 8) // 8, second_grad)

    def weight_grad(first, r):
        d = dh[pl.ds(4 + r, 8), 8 : 8 + W, :].reshape(8 * W, C)
        dt = d.T.astype(BF16)
        terms = []
        for a, b in taps:
            x = window(a1, r + 4 + a * d1, 8 + b * d1, W)
            terms.append(jnp.dot(dt, x, preferred_element_type=F32))
        terms.append(jnp.zeros((C, C), F32))
        for k in range(5):
            value = jnp.concatenate(terms[2 * k : 2 * k + 2], axis=1).reshape(8, 8, LANES)
            if first and k < 4:
                part[8 * k : 8 * k + 8] = value
            else:
                part[8 * k : 8 * k + 8] = part[8 * k : 8 * k + 8] + value

    weight_grad(True, 0)
    if R > 8:
        lax.fori_loop(
            1, R // 8, lambda k, z: (weight_grad(False, pl.multiple_of(k * 8, 8)), z)[1], 0
        )

    sent[...] = part[...].reshape(owners, 8 * group, LANES).astype(BF16)

    def scatter(k, carry):
        target = lax.div(k * n, owners)

        @pl.when(target != me)
        def _():
            pltpu.make_async_remote_copy(
                src_ref=sent.at[k], dst_ref=gath.at[me],
                send_sem=send_s.at[4], recv_sem=recv_s.at[4],
                device_id=device(target), device_id_type=MESH,
            ).start()

        @pl.when(target == me)
        def _():
            gath[me] = sent[k]

        return carry

    lax.fori_loop(0, owners, scatter, 0)

    def input_grad(r):
        total = None
        for t, (a, b) in enumerate(taps):
            x = window(dh, r + 4 - a * d1, 8 - b * d1, W)
            term = jnp.dot(x, w2[t], preferred_element_type=F32)
            total = term if total is None else total + term
        ga[pl.ds(r, 8)] = total.reshape(8, W, C)

    blocks(R // 8, input_grad)
    for r in range(R):
        turned[:, r, :] = ga[r].T
    act_out[...] = turned[...].astype(BF16)

    @pl.when(is_owner)
    def _():
        wait_bytes(gath.at[pl.ds(0, n - 1)], recv_s.at[4])
        total = jnp.sum(gath[...].astype(F32), axis=0)
        red[my_owner] = total.astype(BF16)
        to_all((red.at[my_owner], send_s.at[5], recv_s.at[5]))
        wait_bytes(red.at[pl.ds(0, owners - 1)], recv_s.at[5])

    @pl.when(jnp.logical_not(is_owner))
    def _():
        wait_bytes(red, recv_s.at[5])

    sums = red[...].astype(F32) * (1.0 / extent)
    grads_out[...] = sums.reshape(5, C, LANES)
    head_out[...] = sums[16:20].reshape(C, LANES)[:, C:].T[:bins, :]

    halo_sent(*pair_spec)
    halo_sent(*h2_spec)
    halo_sent(*du_spec)
    wait_bytes(st1.at[pl.ds(0, n - 1)], send_s.at[0])
    wait_bytes(st2.at[pl.ds(0, n - 1)], send_s.at[1])
    wait_bytes(st3.at[pl.ds(0, n - 1)], send_s.at[3])

    @pl.when(has_self)
    def _():
        wait_bytes(yp.at[pl.ds(0, q - 1)], send_s.at[2])

    @pl.when(jnp.logical_not(has_self))
    def _():
        wait_bytes(yp, send_s.at[2])

    @pl.when(is_owner)
    def _():
        wait_bytes(sent.at[pl.ds(0, owners - 1)], send_s.at[4])
        wait_bytes(gath.at[pl.ds(0, n - 1)], send_s.at[5])

    @pl.when(jnp.logical_not(is_owner))
    def _():
        wait_bytes(sent, send_s.at[4])


def body(
    pair, dilations, mask, labels, conv_first, conv_second,
    norm_gain, norm_shift, head_weight, head_bias,
):
    C, R, W = pair.shape
    K = head_weight.shape[1]
    nr, nc = lax.axis_size("row"), lax.axis_size("col")
    n = nr * nc
    vmem = pl.BlockSpec(memory_space=pltpu.VMEM)
    smem = pl.BlockSpec(memory_space=pltpu.SMEM)
    ring = (R + 8, W + 16, C)
    act, grads, head, bias, norm, loss = pl.pallas_call(
        functools.partial(kernel, (R, W, C, nr, nc)),
        out_shape=(
            jax.ShapeDtypeStruct((C, R, W), BF16),
            jax.ShapeDtypeStruct((5, C, LANES), F32),
            jax.ShapeDtypeStruct((K, C), F32),
            jax.ShapeDtypeStruct((1, K), F32),
            jax.ShapeDtypeStruct((2, C), F32),
            jax.ShapeDtypeStruct((1, 1), F32),
        ),
        in_specs=[smem, smem] + [vmem] * 9,
        out_specs=(vmem,) * 6,
        scratch_shapes=[
            pltpu.VMEM((R, W, C), BF16),
            pltpu.VMEM((C, R, W), F32),
            pltpu.VMEM((R, W, C), F32),
            pltpu.VMEM((R + 8, 1, LANES), F32),
            pltpu.VMEM((W + 16, LANES), F32),
            pltpu.VMEM((R * nr + 16, LANES), F32),
            pltpu.VMEM((R, W, LANES), F32),
            pltpu.VMEM((LANES, C), F32),
            pltpu.VMEM((LANES, C), BF16),
            pltpu.VMEM((2 * LANES, LANES), BF16),
            pltpu.VMEM((1, LANES), F32),
            pltpu.VMEM((R + 16, W + 32, C), BF16),
            pltpu.VMEM((R + 16, W + 32, C), F32),
            pltpu.VMEM(ring, F32),
            pltpu.VMEM(ring, F32),
            pltpu.VMEM(ring, F32),
            pltpu.VMEM(ring, F32),
            pltpu.VMEM(ring, F32),
            pltpu.VMEM((R, W, C), F32),
            pltpu.VMEM((R, W, LANES), F32),
            pltpu.VMEM((W // R, R * R // 2, LANES), BF16),
            pltpu.VMEM((W // R, R * R // 2, LANES), BF16),
            pltpu.VMEM((W * R // 2, 2 * LANES), F32),
            pltpu.VMEM((R, W, LANES), F32),
            pltpu.VMEM((n, 1, LANES), F32),
            pltpu.VMEM((n, 1, LANES), F32),
            pltpu.VMEM((n, 4, LANES), F32),
            pltpu.VMEM((40, 8, LANES), F32),
            pltpu.VMEM((OWNERS, 8 * GROUP, LANES), BF16),
            pltpu.VMEM((n, 8 * GROUP, LANES), BF16),
            pltpu.VMEM((OWNERS, 8 * GROUP, LANES), BF16),
            pltpu.SemaphoreType.DMA((3, 8)),
            pltpu.SemaphoreType.DMA((3, 8)),
            pltpu.SemaphoreType.DMA((6,)),
            pltpu.SemaphoreType.DMA((6,)),
        ],
        compiler_params=pltpu.CompilerParams(
            collective_id=0, has_side_effects=True, vmem_limit_bytes=56 * 1024 * 1024
        ),
    )(
        dilations, mask, mask[None], pair, labels,
        conv_first, conv_second, norm_gain, norm_shift, head_weight.T, head_bias[None],
    )
    grads = grads.reshape(5, C, 2, C).transpose(0, 2, 1, 3).reshape(10, C, C)[:9]
    return loss[0, 0], head.T, bias[0], norm, grads, act


def solution(mesh):
    placed = (P(None, "row", "col"), P(), P(), P("row", "col"), P(), P(), P(), P(), P(), P())
    return jax.shard_map(
        body,
        mesh=mesh,
        in_specs=placed,
        out_specs=(P(), P(), P(), P(), P(), P(None, "row", "col")),
        check_vma=False,
    )
```
